128 devices in a mesh: ctx: 64 (over z, y_hi, x, core), head: 2 (over y_lo).
Axes of the slice: x: 4, y: 4 (y_hi: 2, y_lo: 2; y = y_hi * 2 + y_lo), z: 4, core: 2. Of those that a mesh axis runs over, the one named last changes fastest.
Arguments:
- tokens: bfloat16 [49152, 1024], P('ctx')
- qkv_weight: bfloat16 [1024, 3, 1024], P('ctx', None, 'head'), may hold values from -0.1875 to 0.1875
- grad_attn: bfloat16 [49152, 1024], P('ctx', 'head'), may hold values from -6 to 6
- positions: int32 [49152], P('ctx'), may hold values from 0 to 3145727, as said below
- slopes: float32 [16], P('head'), may hold values from 0.03 to 0.6
Outputs:
- d_tokens: bfloat16 [49152, 1024], P('ctx')
- d_weight: float32 [1024, 3, 1024], P('ctx', None, 'head')
The draws below stay inside these ranges and needn't reach their ends.
Inputs may be any that keep to these rules, and one draw needn't show every extreme that they name: positions rise strictly along the sequence, start at 0 and end at 3145727; neighbours differ by 1 to 127.
All inputs are finite; a program needn't handle non-finite values.
Results may differ from the reference program's by a relative error of at most 0.006.
The reference program's roundings to bfloat16 on the way count: a program that leaves them out, or rounds other values in their place, can miss the bound.
Values may be sent and summed in bfloat16 or wider, within the bound.
No kernel may reach another device: no remote copies, remote signals or barrier semaphores. Data moves between devices by JAX's collectives and lax.ppermute only.
A program may use at most 128 MiB of HBM per device.

```python
import math
import jax
import jax.numpy as jnp
from jax import lax

D = 1024
H = 16
HD = 64
ROWS = 768
TOKENS = 49152


def draw_tokens(key, part):
    key = jax.random.fold_in(key, 11)
    first = jax.random.fold_in(key, 0)
    third = jax.random.fold_in(key, 2)
    blocks = TOKENS // ROWS
    base = jax.random.normal(first, (TOKENS, D), jnp.float32)
    pairing = jax.random.permutation(third, blocks)
    width = D // blocks
    row_block = jnp.arange(TOKENS, dtype=jnp.int32) // ROWS
    col_block = jnp.arange(D, dtype=jnp.int32) // width
    spike = jnp.where(pairing[row_block][:, None] == col_block[None, :], 3.0, 1.0).astype(jnp.float32)
    return (base * spike).astype(jnp.bfloat16)


def draw_positions(key, part):
    key = jax.random.fold_in(key, 23)
    extra = jax.random.randint(key, (TOKENS,), 0, 64, dtype=jnp.int32)
    index = jnp.arange(TOKENS, dtype=jnp.int32)
    extra = jnp.where(index == 0, 0, extra)
    extra = jnp.where(index == TOKENS - 1, 63, extra)
    return (64 * index + extra).astype(jnp.int32)


def block_levels(rng, shape, cuts, smallest, high):
    def one(position, shards_of):
        heights = jax.random.uniform(jax.random.fold_in(jax.random.fold_in(rng, 6), position), (shards_of,), jnp.float32, smallest / len(cuts), high / len(cuts))
        return jnp.repeat(jnp.exp(heights), shape[position] // shards_of).reshape((-1,) + (1,) * (len(shape) - position - 1))

    gain = one(*cuts[0])
    for cut in cuts[1:]:
        gain = gain * one(*cut)
    return gain


def gaussian(key, dims, scale, most, cuts=(), held_as=jnp.bfloat16):
    values = scale * jax.random.normal(key, dims, jnp.float32)
    if cuts:
        values = values * block_levels(key, dims, cuts, -0.22, 0.18)
    return jnp.clip(values, -most, most).astype(held_as)


def setup_inputs(seed: int = 0) -> dict:
    splits = jax.random.split(jax.random.key(seed), 6)
    return {
        "tokens": draw_tokens(jax.random.fold_in(splits[5], 71), 0),
        "qkv_weight": gaussian(splits[1], (D, 3, D), D ** -0.5, 0.1875, ((0, 64), (2, 2))),
        "grad_attn": gaussian(splits[2], (TOKENS, D), 1.0, 6.0, ((0, 64), (1, 2))),
        "positions": draw_positions(jax.random.fold_in(splits[5], 71), 0),
        "slopes": jnp.clip(jnp.exp(math.log(0.6) - 2.9957323 * jax.random.uniform(splits[4], (H,), jnp.float32) ** block_levels(splits[4], (H,), ((0, 2),), -0.2, 0.2)), 0.03, 0.6),
    }


def block_grads(q, k, v, grad_heads, positions, slopes, block):
    half = (TOKENS // ROWS) // 2
    far = jnp.bitwise_xor(block, half).astype(jnp.int32)
    start = (block * ROWS).astype(jnp.int32)
    far_start = (far * ROWS).astype(jnp.int32)
    q_blk = lax.dynamic_slice_in_dim(q, start, ROWS, 0).astype(jnp.float32)
    g_blk = lax.dynamic_slice_in_dim(grad_heads, start, ROWS, 0).astype(jnp.float32)
    k_all = jnp.concatenate([lax.dynamic_slice_in_dim(k, start, ROWS, 0), lax.dynamic_slice_in_dim(k, far_start, ROWS, 0)], 0).astype(jnp.float32)
    v_all = jnp.concatenate([lax.dynamic_slice_in_dim(v, start, ROWS, 0), lax.dynamic_slice_in_dim(v, far_start, ROWS, 0)], 0).astype(jnp.float32)
    pos_q = lax.dynamic_slice_in_dim(positions, start, ROWS, 0)
    pos_all = jnp.concatenate([pos_q, lax.dynamic_slice_in_dim(positions, far_start, ROWS, 0)], 0)
    logd = jnp.log1p(jnp.abs(pos_q[:, None] - pos_all[None, :]).astype(jnp.float32))
    scale = HD ** -0.5
    score = jnp.einsum("qhe,khe->hqk", q_blk, k_all) * scale - slopes[:, None, None] * logd[None]
    top = jnp.max(score, axis=-1, keepdims=True)
    expd = jnp.exp(score - top)
    prob = expd / jnp.sum(expd, axis=-1, keepdims=True)
    prob_round = prob.astype(jnp.bfloat16).astype(jnp.float32)
    outv = jnp.einsum("hqk,khe->qhe", prob_round, v_all)
    delta = jnp.sum(g_blk * outv, axis=-1)
    delta = jnp.transpose(delta)[:, :, None]
    dprob = jnp.einsum("qhe,khe->hqk", g_blk, v_all)
    dscore = (prob * (dprob - delta) * scale).astype(jnp.bfloat16).astype(jnp.float32)
    dq = jnp.einsum("hqk,khe->qhe", dscore, k_all)
    dk = jnp.einsum("hqk,qhe->khe", dscore, q_blk)
    dv = jnp.einsum("hqk,qhe->khe", prob_round, g_blk)
    return dq, dk, dv


def reference(tokens, qkv_weight, grad_attn, positions, slopes):
    nblocks = TOKENS // ROWS
    qkv = jnp.einsum("sd,dcf->scf", tokens.astype(jnp.float32), qkv_weight.astype(jnp.float32)).astype(jnp.bfloat16)
    q = qkv[:, 0].reshape(TOKENS, H, HD)
    k = qkv[:, 1].reshape(TOKENS, H, HD)
    v = qkv[:, 2].reshape(TOKENS, H, HD)
    grad_heads = grad_attn.reshape(TOKENS, H, HD)

    def one_block(block):
        return block_grads(q, k, v, grad_heads, positions, slopes, block)

    dq, dk_all, dv_all = lax.map(one_block, jnp.arange(nblocks, dtype=jnp.int32))
    paired = jnp.bitwise_xor(jnp.arange(nblocks, dtype=jnp.int32), nblocks // 2)
    dk = dk_all[:, :ROWS] + dk_all[paired, ROWS:]
    dv = dv_all[:, :ROWS] + dv_all[paired, ROWS:]
    dqkv = jnp.stack([dq.reshape(TOKENS, D).astype(jnp.bfloat16), dk.reshape(TOKENS, D).astype(jnp.bfloat16), dv.reshape(TOKENS, D).astype(jnp.bfloat16)], 1)
    dqkv_wide = dqkv.astype(jnp.float32)
    d_tokens = jnp.einsum("scf,dcf->sd", dqkv_wide, qkv_weight.astype(jnp.float32)).astype(jnp.bfloat16)
    d_weight = jnp.einsum("sd,scf->dcf", tokens.astype(jnp.float32), dqkv_wide)
    return d_tokens, d_weight
```

```python
import jax
import jax.numpy as jnp
from jax import lax
from jax.experimental import pallas as pl
from jax.experimental.pallas import tpu as pltpu
from jax.sharding import PartitionSpec as P

BF = jnp.bfloat16
F32 = jnp.float32
TILE = 256


def swap(value, axis):
    return lax.ppermute(value, axis, [(0, 1), (1, 0)])


def dot(a, b, dims=((1,), (0,))):
    return lax.dot_general(a, b, (dims, ((), ())), preferred_element_type=F32)


def attention_kernel(
    slopes_ref, qo, qf, ko, kf, vo, vf, go, gf, logd_ref, near_ref, far_ref,
    q_s, k_s, v_s, g_s, kt_s, dk_s, dv_s, s_s, dp_s,
):
    step = pl.program_id(0)
    rows = qo.shape[0]
    total = 2 * rows
    chunks = total // TILE

    @pl.when(step == 0)
    def _():
        for scratch, near, far in ((q_s, qo, qf), (k_s, ko, kf), (v_s, vo, vf), (g_s, go, gf)):
            scratch[:rows] = near[...]
            scratch[rows:] = far[...]
        kt_s[...] = k_s[...].astype(F32).T.astype(BF)
        dk_s[...] = jnp.zeros_like(dk_s)
        dv_s[...] = jnp.zeros_like(dv_s)

    here = pl.ds(pl.multiple_of(step * TILE, TILE), TILE)
    q = (q_s[here].astype(F32) * 0.125)
    g = g_s[here].astype(F32)
    q_t, g_t = q.T, g.T
    upper = lax.broadcasted_iota(jnp.int32, (128, TILE), 0) < 64
    left = lax.broadcasted_iota(jnp.int32, (TILE, 128), 1) < 64
    zero = jnp.float32(0)
    qts = [jnp.where(upper, q_t, zero).astype(BF), jnp.where(upper, zero, q_t).astype(BF)]
    gts = [jnp.where(upper, g_t, zero).astype(BF), jnp.where(upper, zero, g_t).astype(BF)]
    qs = [jnp.where(left, q, zero).astype(BF), jnp.where(left, zero, q).astype(BF)]
    gs = [jnp.where(left, g, zero).astype(BF), jnp.where(left, zero, g).astype(BF)]
    for h in range(2):
        slope = slopes_ref[h]
        top = None
        for c in range(chunks):
            part = slice(c * TILE, (c + 1) * TILE)
            score = dot(k_s[part], qts[h]) - slope * logd_ref[part]
            s_s[h, part] = score
            peak = jnp.max(score, axis=0, keepdims=True)
            top = peak if top is None else jnp.maximum(top, peak)
        norm = jnp.zeros((1, TILE), F32)
        delta = jnp.zeros((1, TILE), F32)
        for c in range(chunks):
            part = slice(c * TILE, (c + 1) * TILE)
            e = jnp.exp(s_s[h, part] - top)
            s_s[h, part] = e
            dp = dot(v_s[part], gts[h])
            dp_s[h, part] = dp
            norm += jnp.sum(e, axis=0, keepdims=True)
            delta += jnp.sum(e * dp, axis=0, keepdims=True)
        inverse = 1.0 / norm
        delta = delta * inverse
        dq_t = jnp.zeros((64, TILE), F32)
        for c in range(chunks):
            part = slice(c * TILE, (c + 1) * TILE)
            p = s_s[h, part] * inverse
            ds = (p * (dp_s[h, part] - delta)).astype(BF)
            dv_s[part] += dot(p.astype(BF), gs[h])
            dk_s[part] += dot(ds, qs[h])
            dq_t += dot(kt_s[h * 64 : (h + 1) * 64, part], ds)
        s_s[h, :64] = dq_t
    dq = jnp.concatenate([s_s[0, :64], s_s[1, :64]], 0).T * 0.125
    local = pl.ds(pl.multiple_of(lax.rem(step, chunks // 2) * TILE, TILE), TILE)

    @pl.when(step < chunks // 2)
    def _():
        near_ref[local, :128] = dq.astype(BF)

    @pl.when(step >= chunks // 2)
    def _():
        far_ref[local, :128] = dq.astype(BF)

    @pl.when(step == chunks - 1)
    def _():
        near_ref[:, 128:256] = dk_s[:rows].astype(BF)
        near_ref[:, 256:384] = dv_s[:rows].astype(BF)
        far_ref[:, 128:256] = dk_s[rows:].astype(BF)
        far_ref[:, 256:384] = dv_s[rows:].astype(BF)


def attention(slopes, near, far, g_near, g_far, logd, pair):
    rows = near.shape[0]
    total = 2 * rows

    def column(block):
        return pl.BlockSpec((rows, 128), lambda t: (0, block))

    specs = []
    for c in range(3):
        specs += [column(3 * pair + c)] * 2
    return pl.pallas_call(
        attention_kernel,
        grid=(total // TILE,),
        in_specs=[pl.BlockSpec(memory_space=pltpu.SMEM)]
        + specs
        + [column(pair)] * 2
        + [pl.BlockSpec((total, TILE), lambda t: (0, t))],
        out_specs=[pl.BlockSpec((rows, 384), lambda t: (0, 0))] * 2,
        out_shape=[jax.ShapeDtypeStruct((rows, 384), BF)] * 2,
        scratch_shapes=[pltpu.VMEM((total, 128), BF)] * 4
        + [pltpu.VMEM((128, total), BF)]
        + [pltpu.VMEM((total, 128), F32)] * 2
        + [pltpu.VMEM((2, total, TILE), F32)] * 2,
        compiler_params=pltpu.CompilerParams(vmem_limit_bytes=32 * 2**20),
        cost_estimate=pl.CostEstimate(
            flops=2 * 5 * 2 * total * total * 256, bytes_accessed=4 * total * total, transcendentals=2 * total * total
        ),
    )(slopes, near, far, near, far, near, far, g_near, g_far, logd)


def by_core(own, other, core):
    stack = jnp.where(core == 0, jnp.stack([own, other], 1), jnp.stack([other, own], 1))
    return stack.reshape(1024, own.shape[2])


def own_core_first(array, core):
    split = array.reshape(32, 2, 16, array.shape[1])
    first, second = split[:, 0], split[:, 1]
    first, second = jnp.where(core == 0, first, second), jnp.where(core == 0, second, first)
    return jnp.concatenate([first.reshape(512, -1), second.reshape(512, -1)], 0)


def on_device(tokens, qkv_weight, grad_attn, positions, slopes):
    z_hi, core, head = lax.axis_index("zh"), lax.axis_index("c"), lax.axis_index("h")
    rows = tokens.shape[0]
    half, quarter = rows // 2, rows // 4

    with jax.named_scope("tokens"):
        send = [lax.dynamic_slice_in_dim(tokens, head * half + i * quarter, quarter, 0) for i in range(2)]
        got = [swap(part, "zh") for part in send]
        other = [swap(part, "h") for part in got]
        far_tokens = jnp.where(
            head == 0, jnp.concatenate(got + other, 0), jnp.concatenate(other + got, 0)
        )

    with jax.named_scope("weights"):
        w = qkv_weight.reshape(16, 3, 2, 2, 128).transpose(2, 0, 3, 1, 4).reshape(2, 1, 16, 768)
        w = jnp.broadcast_to(w, (2, 16, 16, 768)).reshape(32, 16, 768)
        w = lax.all_to_all(w, ("zh", "zl", "yh", "x"), 0, 0)
        w = by_core(w, swap(w, "c"), core)

    with jax.named_scope("bias"):
        g_near = lax.dynamic_slice_in_dim(grad_attn, z_hi * 256, 256, 1)
        g_far = swap(lax.dynamic_slice_in_dim(grad_attn, (1 - z_hi) * 256, 256, 1), "zh")
        pos = jnp.concatenate([positions, swap(positions, "zh")], 0)
        logd = jnp.log((1 + jnp.abs(pos[:, None] - pos[None, :])).astype(F32))
        slopes = lax.dynamic_slice_in_dim(slopes, z_hi * 4, 4, 0)

    with jax.named_scope("transposed"):
        near_t = own_core_first(tokens.T, core)
        far_t = own_core_first(far_tokens.T, core)
        near_t, far_t = lax.optimization_barrier((near_t, far_t))

    with jax.named_scope("projection"):
        near = dot(tokens, w).astype(BF)
        far = dot(far_tokens, w).astype(BF)
    with jax.named_scope("attention"):
        grads = [attention(slopes[2 * p : 2 * p + 2], near, far, g_near, g_far, logd, p) for p in range(2)]

    with jax.named_scope("d_tokens"):
        w_other = swap(w, "zh")
        total = 0.0
        for p in range(2):
            part = slice(384 * p, 384 * (p + 1))
            back = swap(grads[p][1], "zh")
            total = total + dot(grads[p][0], w[:, part], ((1,), (1,)))
            total = total + dot(back, w_other[:, part], ((1,), (1,)))
        total = total.astype(BF)
        outs = []
        for i in range(2):
            mine = total[i * half : (i + 1) * half]
            outs.append((mine.astype(F32) + swap(mine, "h").astype(F32)).astype(BF))
        d_tokens = jnp.concatenate(outs, 0)

    with jax.named_scope("d_weight"):
        terms = []
        for p in range(2):
            term = dot(near_t, grads[p][0]) + dot(far_t, grads[p][1])
            terms.append((term[:512] + swap(term[512:], "c")).astype(BF))
        term = jnp.concatenate(terms, 1).reshape(32, 16, 768)
        term = lax.all_to_all(term, ("zh", "zl", "yh", "x"), 0, 0)
        term = jnp.sum(term.reshape(2, 16, 16, 768).astype(F32), axis=1)
        d_weight = term.reshape(2, 16, 2, 3, 128).transpose(1, 3, 0, 2, 4).reshape(16, 3, 512)
    return d_tokens, d_weight


def solution(mesh):
    mesh = jax.sharding.Mesh(mesh.devices.reshape(2, 2, 2, 4, 2, 2), ("zh", "zl", "yh", "x", "c", "h"))
    ctx = ("zh", "zl", "yh", "x", "c")
    return jax.shard_map(
        on_device,
        mesh=mesh,
        in_specs=(P(ctx, None), P(ctx, None, "h"), P(ctx, "h"), P(ctx), P("h")),
        out_specs=(P(ctx, None), P(ctx, None, "h")),
        check_vma=False,
    )
```

```python
import jax
import jax.numpy as jnp
from jax import lax
from jax.experimental import pallas as pl
from jax.experimental.pallas import tpu as pltpu
from jax.sharding import PartitionSpec as P

BF = jnp.bfloat16
F32 = jnp.float32
TILE = 256


def swap(value, axis):
    return lax.ppermute(value, axis, [(0, 1), (1, 0)])


def dot(a, b, dims=((1,), (0,))):
    return lax.dot_general(a, b, (dims, ((), ())), preferred_element_type=F32)


def attention_kernel(
    place_ref, slopes_ref, qo, qf, ko, kf, vo, vf, go, gf, logd_ref, near_ref, *rest,
):
    *far_refs, q_s, k_s, v_s, g_s, kt_s, dk_s, dv_s, s_s, dp_s = rest
    step = pl.program_id(0)
    rows = qo.shape[0]
    total = 2 * rows
    chunks = total // TILE

    @pl.when(step == 0)
    def _():
        for scratch, near, far in ((q_s, qo, qf), (k_s, ko, kf), (v_s, vo, vf), (g_s, go, gf)):
            scratch[:rows] = near[...]
            scratch[rows:] = far[...]
        kt_s[...] = k_s[...].astype(F32).T.astype(BF)
        dk_s[...] = jnp.zeros_like(dk_s)
        dv_s[...] = jnp.zeros_like(dv_s)

    here = pl.ds(pl.multiple_of(step * TILE, TILE), TILE)
    q = (q_s[here].astype(F32) * 0.125)
    g = g_s[here].astype(F32)
    q_t, g_t = q.T, g.T
    upper = lax.broadcasted_iota(jnp.int32, (128, TILE), 0) < 64
    left = lax.broadcasted_iota(jnp.int32, (TILE, 128), 1) < 64
    zero = jnp.float32(0)
    qts = [jnp.where(upper, q_t, zero).astype(BF), jnp.where(upper, zero, q_t).astype(BF)]
    gts = [jnp.where(upper, g_t, zero).astype(BF), jnp.where(upper, zero, g_t).astype(BF)]
    qs = [jnp.where(left, q, zero).astype(BF), jnp.where(left, zero, q).astype(BF)]
    gs = [jnp.where(left, g, zero).astype(BF), jnp.where(left, zero, g).astype(BF)]
    for h in range(2):
        slope = slopes_ref[h]
        top = None
        for c in range(chunks):
            part = slice(c * TILE, (c + 1) * TILE)
            score = dot(k_s[part], qts[h]) - slope * logd_ref[part]
            s_s[h, part] = score
            peak = jnp.max(score, axis=0, keepdims=True)
            top = peak if top is None else jnp.maximum(top, peak)
        norm = jnp.zeros((1, TILE), F32)
        delta = jnp.zeros((1, TILE), F32)
        for c in range(chunks):
            part = slice(c * TILE, (c + 1) * TILE)
            e = jnp.exp(s_s[h, part] - top)
            s_s[h, part] = e
            dp = dot(v_s[part], gts[h])
            dp_s[h, part] = dp
            norm += jnp.sum(e, axis=0, keepdims=True)
            delta += jnp.sum(e * dp, axis=0, keepdims=True)
        inverse = 1.0 / norm
        delta = delta * inverse
        dq_t = jnp.zeros((64, TILE), F32)
        for c in range(chunks):
            part = slice(c * TILE, (c + 1) * TILE)
            p = s_s[h, part] * inverse
            ds = (p * (dp_s[h, part] - delta)).astype(BF)
            dv_s[part] += dot(p.astype(BF), gs[h])
            dk_s[part] += dot(ds, qs[h])
            dq_t += dot(kt_s[h * 64 : (h + 1) * 64, part], ds)
        s_s[h, :64] = dq_t
    dq = jnp.concatenate([s_s[0, :64], s_s[1, :64]], 0).T * 0.125
    @pl.when(step < chunks // 2)
    def _():
        near_ref[here, :128] = dq.astype(BF)

    @pl.when(step >= chunks // 2)
    def _():
        q_s[here] = dq.astype(BF)

    @pl.when(step == chunks - 1)
    def _():
        near_ref[:, 128:256] = dk_s[:rows].astype(BF)
        near_ref[:, 256:384] = dv_s[:rows].astype(BF)
        third = rows // 3
        first = 0
        for far_ref in far_refs:
            for k in range(far_ref.shape[0] // third):
                at = (first + k) ^ place_ref[0] if first + k < 2 else first + k
                part = pl.ds(pl.multiple_of(rows + at * third, 64), third)
                mine = slice(k * third, (k + 1) * third)
                far_ref[mine, :128] = q_s[part]
                far_ref[mine, 128:256] = dk_s[part].astype(BF)
                far_ref[mine, 256:384] = dv_s[part].astype(BF)
            first += far_ref.shape[0] // third


def attention(place, slopes, near, far, g_near, g_far, logd, pair, pieces):
    rows = near.shape[0]
    total = 2 * rows
    sizes = [rows] + pieces

    def column(block):
        return pl.BlockSpec((rows, 128), lambda t: (0, block))

    specs = []
    for c in range(3):
        specs += [column(3 * pair + c)] * 2
    return pl.pallas_call(
        attention_kernel,
        grid=(total // TILE,),
        in_specs=[pl.BlockSpec(memory_space=pltpu.SMEM)] * 2
        + specs
        + [column(pair)] * 2
        + [pl.BlockSpec((total, TILE), lambda t: (0, t))],
        out_specs=[pl.BlockSpec((n, 384), lambda t: (0, 0)) for n in sizes],
        out_shape=[jax.ShapeDtypeStruct((n, 384), BF) for n in sizes],
        scratch_shapes=[pltpu.VMEM((total, 128), BF)] * 4
        + [pltpu.VMEM((128, total), BF)]
        + [pltpu.VMEM((total, 128), F32)] * 2
        + [pltpu.VMEM((2, total, TILE), F32)] * 2,
        compiler_params=pltpu.CompilerParams(vmem_limit_bytes=32 * 2**20),
        cost_estimate=pl.CostEstimate(
            flops=2 * 5 * 2 * total * total * 256, bytes_accessed=4 * total * total, transcendentals=2 * total * total
        ),
    )(place[None], slopes, near, far, near, far, near, far, g_near, g_far, logd)


def add_kernel(mine_ref, theirs_ref, *refs):
    refs[-1][...] = (mine_ref[...].astype(F32) + theirs_ref[...].astype(F32)).astype(BF)


def add_rows(out, mine, theirs, index, count):
    rows, width = mine.shape
    return pl.pallas_call(
        add_kernel,
        grid=(1,),
        in_specs=[pl.BlockSpec((rows, width), lambda i: (0, 0))] * 2
        + ([] if out is None else [pl.BlockSpec(memory_space=pl.ANY)]),
        out_specs=pl.BlockSpec((rows, width), lambda i: (index, 0)),
        out_shape=jax.ShapeDtypeStruct((rows * count, width), BF),
        input_output_aliases={} if out is None else {2: 0},
        cost_estimate=pl.CostEstimate(flops=1000, bytes_accessed=1000, transcendentals=0),
    )(mine, theirs, *([] if out is None else [out]))


def weight_kernel(place_ref, near_ref, far_ref, *refs):
    *grads, keep_ref, send_ref, term_s = refs
    core, x, head = place_ref[0], place_ref[1], place_ref[2]
    step = pl.program_id(0)
    third = far_ref.shape[0] // 3
    for p in range(len(grads) // 2):
        near = lax.dot_general(near_ref[...], grads[2 * p][...], (((0,), (0,)), ((), ())), preferred_element_type=F32)
        for k in range(3):
            at = k ^ head if k < 2 else k
            part = pl.ds(pl.multiple_of(at * third, 64), third)
            near += lax.dot_general(
                far_ref[k * third : (k + 1) * third],
                grads[2 * p + 1][part],
                (((0,), (0,)), ((), ())),
                preferred_element_type=F32,
            )
        term_s[:, p * 384 : (p + 1) * 384] = near
    groups = term_s.shape[0] // 128
    for i in range(groups):
        for j in range(4):
            to = pl.ds(pl.multiple_of((j * 8 + step * groups + i) * 16, 16), 16)
            at = 128 * i + 32 * (j ^ x)
            keep_ref[to] = term_s[pl.ds(pl.multiple_of(at + 16 * core, 16), 16)]
            send_ref[to] = term_s[pl.ds(pl.multiple_of(at + 16 * (1 - core), 16), 16)]


def weight_terms(place, near, far, grads):
    rows, width = near.shape
    columns = 192 * len(grads)
    tile = 256
    whole = pl.BlockSpec((rows, 384), lambda i: (0, 0))
    return pl.pallas_call(
        weight_kernel,
        grid=(width // tile,),
        in_specs=[pl.BlockSpec(memory_space=pltpu.SMEM)]
        + [pl.BlockSpec((rows, tile), lambda i: (0, i))] * 2
        + [whole] * len(grads),
        out_specs=[pl.BlockSpec((width // 2, columns), lambda i: (0, 0))] * 2,
        out_shape=[jax.ShapeDtypeStruct((width // 2, columns), F32)] * 2,
        scratch_shapes=[pltpu.VMEM((tile, columns), F32)],
        compiler_params=pltpu.CompilerParams(vmem_limit_bytes=32 * 2**20),
        cost_estimate=pl.CostEstimate(flops=1000, bytes_accessed=1000, transcendentals=0),
    )(place, near, far, *grads)


def pick(array, place, dim):
    first = lax.index_in_dim(array, 0, dim, keepdims=False)
    second = lax.index_in_dim(array, 1, dim, keepdims=False)
    return jnp.where(place == 0, first, second), jnp.where(place == 0, second, first)


def ordered(own, other, place):
    return jnp.where(place == 0, jnp.concatenate([own, other], 0), jnp.concatenate([other, own], 0))


def on_device(tokens, qkv_weight, grad_attn, positions, slopes):
    z_hi, z_lo, y_hi = lax.axis_index("zh"), lax.axis_index("zl"), lax.axis_index("yh")
    x, core, head = lax.axis_index("x"), lax.axis_index("c"), lax.axis_index("h")
    rows = tokens.shape[0]
    third = rows // 3

    def local(array):
        first, second = array[:third], array[third : 2 * third]
        return jnp.where(head == 0, array, jnp.concatenate([second, first, array[2 * third :]], 0))

    with jax.named_scope("tokens"):
        got = [swap(lax.dynamic_slice_in_dim(tokens, head * third, third, 0), "zh"), swap(tokens[2 * third :], "zh")]

    with jax.named_scope("weights"):
        w = qkv_weight.reshape(16, 3, 2, 2, 128).transpose(2, 0, 3, 1, 4).reshape(2, 16, 768)
        mine = lax.dynamic_index_in_dim(w, z_hi, 0, keepdims=False)
        theirs = lax.dynamic_index_in_dim(w, 1 - z_hi, 0, keepdims=False)
        digits = jnp.stack([(positions >> shift) & 255 for shift in (16, 8, 0)]).astype(BF)
        other = lax.ppermute(jnp.concatenate([theirs, digits], 0), ("zh", "zl"), [(i, i ^ 2) for i in range(4)])
        pieces = [
            mine,
            lax.ppermute(mine, ("zh", "zl"), [(i, i ^ 1) for i in range(4)]),
            other[:16],
            lax.ppermute(theirs, ("zh", "zl"), [(i, i ^ 3) for i in range(4)]),
        ]
        digits = other[16:].astype(jnp.int32)
        far_positions = local((digits[0] << 16) + (digits[1] << 8) + digits[2])
        pos = jnp.concatenate([positions, far_positions], 0)
        logd = jnp.log((1 + jnp.abs(pos[:, None] - pos[None, :])).astype(F32))
        pieces = [jnp.where(z_lo == 0, pieces[i], pieces[i ^ 1]) for i in range(4)]
        pieces = [jnp.where(z_hi == 0, pieces[i], pieces[i ^ 2]) for i in range(4)]
        w, grad_attn = lax.optimization_barrier((jnp.stack(pieces)[:, None], grad_attn))
        other = swap(w, "yh")
        w = jnp.where(y_hi == 0, jnp.concatenate([w, other], 1), jnp.concatenate([other, w], 1)).reshape(8, 16, 768)
        w, got[0], logd = lax.optimization_barrier((w, got[0], logd))
        relayed = swap(got[0], "h")
        pieces = [w] + [lax.ppermute(w, "x", [(i, i ^ j) for i in range(4)]) for j in range(1, 4)]
        pieces = [jnp.where((x & 1) == 0, pieces[i], pieces[i ^ 1]) for i in range(4)]
        pieces = [jnp.where((x & 2) == 0, pieces[i], pieces[i ^ 2]) for i in range(4)]
        w = jnp.stack(pieces, 1)
        other = swap(w, "c")
        w = jnp.where(core == 0, jnp.stack([w, other], 2), jnp.stack([other, w], 2)).reshape(1024, 768)
        far_tokens = jnp.concatenate([got[0], relayed, got[1]], 0)

    with jax.named_scope("bias"):
        g_near = lax.dynamic_slice_in_dim(grad_attn, z_hi * 256, 256, 1)
        g_far = swap(local(lax.dynamic_slice_in_dim(grad_attn, (1 - z_hi) * 256, 256, 1)), "zh")
        slopes = lax.dynamic_slice_in_dim(slopes, z_hi * 4, 4, 0)

    with jax.named_scope("projection"):
        near = dot(tokens, w).astype(BF)
        far = dot(far_tokens, w).astype(BF)
    with jax.named_scope("attention"):
        near0, far0 = attention(head, slopes[:2], near, far, g_near, g_far, logd, 0, [rows])
        g_near, near0 = lax.optimization_barrier((g_near, near0))
        near1, *far1 = attention(head, slopes[2:], near, far, g_near, g_far, logd, 1, [third, 2 * third])

    with jax.named_scope("d_tokens"):
        w_other = swap(w, "zh")
        back0 = swap(far0, "zh")
        back1 = [swap(part, "zh") for part in far1]
        base = dot(
            jnp.concatenate([near0, near1, back0], 1), jnp.concatenate([w, w_other[:, :384]], 1), ((1,), (1,))
        )
        mine = []
        for i in range(3):
            back = back1[0] if i == 0 else back1[1][(i - 1) * third : i * third]
            part = base[i * third : (i + 1) * third] + dot(back, w_other[:, 384:], ((1,), (1,)))
            mine.append(part.astype(BF))

    with jax.named_scope("d_weight"):
        far1 = jnp.concatenate(far1, 0)
        far1, back0 = lax.optimization_barrier((far1, back0))
        keep, send = weight_terms(jnp.stack([core, x, head]), tokens, far_tokens, [near0, far0, near1, far1])
        other = swap(send, "c")
        theirs = [swap(mine[0], "h")]
        other, theirs[0] = lax.optimization_barrier((other, theirs[0]))
        term = (keep + other).reshape(4, 8, 16, 768)
        total = term[0]
        for j in range(1, 4):
            piece = lax.ppermute(term[j].astype(BF), "x", [(i, i ^ j) for i in range(4)])
            total = total + piece.astype(F32)
        total = total.reshape(2, 2, 2, 16, 768)
        theirs.append(swap(mine[1], "h"))
        total, theirs[1], mine[2] = lax.optimization_barrier((total, theirs[1], mine[2]))
        theirs.append(swap(mine[2], "h"))
        mine_w, their_w = pick(total, y_hi, 2)
        total = mine_w + swap(their_w.astype(BF), "yh").astype(F32)
        halves = []
        for a in range(2):
            part = total if a == 0 else total[::-1]
            part = jnp.where(z_hi == 0, part[0], part[1])
            mine_w, their_w = pick(part, z_lo, 0)
            if a:
                mine_w = lax.ppermute(mine_w, ("zh", "zl"), [(i, i ^ 2) for i in range(4)])
            halves.append(mine_w + lax.ppermute(their_w, ("zh", "zl"), [(i, i ^ (2 * a + 1)) for i in range(4)]))
        total = jnp.where(z_hi == 0, jnp.stack(halves), jnp.stack(halves[::-1]))
        d_weight = total.reshape(2, 16, 2, 3, 128).transpose(1, 3, 0, 2, 4).reshape(16, 3, 512)

    with jax.named_scope("d_tokens"):
        d_tokens = None
        for i in range(3):
            d_tokens = add_rows(d_tokens, mine[i], theirs[i], i, 3)
    return d_tokens, d_weight


def solution(mesh):
    mesh = jax.sharding.Mesh(mesh.devices.reshape(2, 2, 2, 4, 2, 2), ("zh", "zl", "yh", "x", "c", "h"))
    ctx = ("zh", "zl", "yh", "x", "c")
    return jax.shard_map(
        on_device,
        mesh=mesh,
        in_specs=(P(ctx, None), P(ctx, None, "h"), P(ctx, "h"), P(ctx), P("h")),
        out_specs=(P(ctx, None), P(ctx, None, "h")),
        check_vma=False,
    )
```

```python
import jax
import jax.numpy as jnp
from jax import lax
from jax.experimental import pallas as pl
from jax.experimental.pallas import tpu as pltpu
from jax.sharding import PartitionSpec as P

BF = jnp.bfloat16
F32 = jnp.float32
TILE = 512
CHUNK = 128


def swap(value, axis):
    return lax.ppermute(value, axis, [(0, 1), (1, 0)])


def dot(a, b, dims=((1,), (0,))):
    return lax.dot_general(a, b, (dims, ((), ())), preferred_element_type=F32)


def attention_kernel(
    place_ref, slopes_ref, qo, qf, ko, kf, vo, vf, go, gf, logd_ref, near_ref, *rest,
):
    *far_refs, q_s, k_s, v_s, g_s, kt_s, dq_s, dk_s, dv_s, s_s, dp_s = rest
    step = pl.program_id(0)
    rows = qo.shape[0]
    total = 2 * rows
    steps = total // TILE

    @pl.when(step == 0)
    def _():
        for scratch, near, far in ((q_s, qo, qf), (k_s, ko, kf), (v_s, vo, vf), (g_s, go, gf)):
            scratch[:rows] = near[...]
            scratch[rows:] = far[...]
        kt_s[...] = k_s[...].astype(F32).T.astype(BF)
        dk_s[...] = jnp.zeros_like(dk_s)
        dv_s[...] = jnp.zeros_like(dv_s)

    here = pl.ds(pl.multiple_of(step * TILE, TILE), TILE)
    q = q_s[here].astype(F32) * 0.125
    g = g_s[here].astype(F32)
    q_t, g_t = q.T, g.T
    upper = lax.broadcasted_iota(jnp.int32, (128, TILE), 0) < 64
    left = lax.broadcasted_iota(jnp.int32, (TILE, 128), 1) < 64
    zero = jnp.float32(0)
    qts = [jnp.where(upper, q_t, zero).astype(BF), jnp.where(upper, zero, q_t).astype(BF)]
    gts = [jnp.where(upper, g_t, zero).astype(BF), jnp.where(upper, zero, g_t).astype(BF)]
    qs = [jnp.where(left, q, zero).astype(BF), jnp.where(left, zero, q).astype(BF)]
    gs = [jnp.where(left, g, zero).astype(BF), jnp.where(left, zero, g).astype(BF)]
    top = [jnp.full((1, TILE), -jnp.inf, F32)] * 2
    norm = [jnp.zeros((1, TILE), F32)] * 2
    delta = [jnp.zeros((1, TILE), F32)] * 2
    inverse = [None] * 2
    dq_t = [jnp.zeros((64, TILE), F32)] * 2
    parts = [slice(c * CHUNK, (c + 1) * CHUNK) for c in range(total // CHUNK)]

    def scores(h, part):
        score = dot(k_s[part], qts[h]) - slopes_ref[h] * logd_ref[part]
        s_s[h, part] = score
        top[h] = jnp.maximum(top[h], jnp.max(score, axis=0, keepdims=True))

    def sums(h, part):
        e = jnp.exp(s_s[h, part] - top[h])
        s_s[h, part] = e
        dp = dot(v_s[part], gts[h])
        dp_s[h, part] = dp
        norm[h] += jnp.sum(e, axis=0, keepdims=True)
        delta[h] += jnp.sum(e * dp, axis=0, keepdims=True)

    def normalise(h):
        inverse[h] = 1.0 / norm[h]
        delta[h] = delta[h] * inverse[h]

    def products(h, part):
        p = s_s[h, part] * inverse[h]
        ds = (p * (dp_s[h, part] - delta[h])).astype(BF)
        dv_s[part] += dot(p.astype(BF), gs[h])
        dk_s[part] += dot(ds, qs[h])
        dq_t[h] += dot(kt_s[h * 64 : (h + 1) * 64, part], ds)

    for part in parts:
        scores(0, part)
    for part in parts:
        sums(0, part)
        scores(1, part)
    normalise(0)
    for part in parts:
        products(0, part)
        sums(1, part)
    normalise(1)
    for part in parts:
        products(1, part)
    dq = jnp.concatenate(dq_t, 0).T * 0.125
    dq_s[here] = dq.astype(BF)

    @pl.when(step == steps - 1)
    def _():
        near_ref[:, :128] = dq_s[:rows]
        near_ref[:, 128:256] = dk_s[:rows].astype(BF)
        near_ref[:, 256:384] = dv_s[:rows].astype(BF)
        third = rows // 3
        first = 0
        for far_ref in far_refs:
            for k in range(far_ref.shape[0] // third):
                at = (first + k) ^ place_ref[0] if first + k < 2 else first + k
                part = pl.ds(pl.multiple_of(rows + at * third, 64), third)
                mine = slice(k * third, (k + 1) * third)
                far_ref[mine, :128] = dq_s[part]
                far_ref[mine, 128:256] = dk_s[part].astype(BF)
                far_ref[mine, 256:384] = dv_s[part].astype(BF)
            first += far_ref.shape[0] // third


def attention(place, slopes, near, far, g_near, g_far, logd, pair, pieces):
    rows = near.shape[0]
    total = 2 * rows
    sizes = [rows] + pieces

    def column(block):
        return pl.BlockSpec((rows, 128), lambda t: (0, block))

    specs = []
    for c in range(3):
        specs += [column(3 * pair + c)] * 2
    return pl.pallas_call(
        attention_kernel,
        grid=(total // TILE,),
        in_specs=[pl.BlockSpec(memory_space=pltpu.SMEM)] * 2
        + specs
        + [column(pair)] * 2
        + [pl.BlockSpec((total, TILE), lambda t: (0, t))],
        out_specs=[pl.BlockSpec((n, 384), lambda t: (0, 0)) for n in sizes],
        out_shape=[jax.ShapeDtypeStruct((n, 384), BF) for n in sizes],
        scratch_shapes=[pltpu.VMEM((total, 128), BF)] * 4
        + [pltpu.VMEM((128, total), BF), pltpu.VMEM((total, 128), BF)]
        + [pltpu.VMEM((total, 128), F32)] * 2
        + [pltpu.VMEM((2, total, TILE), F32)] * 2,
        compiler_params=pltpu.CompilerParams(vmem_limit_bytes=44 * 2**20),
        cost_estimate=pl.CostEstimate(
            flops=2 * 5 * 2 * total * total * 256, bytes_accessed=4 * total * total, transcendentals=2 * total * total
        ),
    )(place[None], slopes, near, far, near, far, near, far, g_near, g_far, logd)


def add_kernel(mine_ref, theirs_ref, *refs):
    refs[-1][...] = (mine_ref[...].astype(F32) + theirs_ref[...].astype(F32)).astype(BF)


def add_rows(out, mine, theirs, index, count):
    rows, width = mine.shape
    return pl.pallas_call(
        add_kernel,
        grid=(1,),
        in_specs=[pl.BlockSpec((rows, width), lambda i: (0, 0))] * 2
        + ([] if out is None else [pl.BlockSpec(memory_space=pl.ANY)]),
        out_specs=pl.BlockSpec((rows, width), lambda i: (index, 0)),
        out_shape=jax.ShapeDtypeStruct((rows * count, width), BF),
        input_output_aliases={} if out is None else {2: 0},
        cost_estimate=pl.CostEstimate(flops=1000, bytes_accessed=1000, transcendentals=0),
    )(mine, theirs, *([] if out is None else [out]))


def weight_kernel(place_ref, near_ref, far_ref, *refs):
    *grads, keep_ref, send_ref, term_s = refs
    core, x, head = place_ref[0], place_ref[1], place_ref[2]
    step = pl.program_id(0)
    third = far_ref.shape[0] // 3
    for p in range(len(grads) // 2):
        near = lax.dot_general(near_ref[...], grads[2 * p][...], (((0,), (0,)), ((), ())), preferred_element_type=F32)
        for k in range(3):
            at = k ^ head if k < 2 else k
            part = pl.ds(pl.multiple_of(at * third, 64), third)
            near += lax.dot_general(
                far_ref[k * third : (k + 1) * third],
                grads[2 * p + 1][part],
                (((0,), (0,)), ((), ())),
                preferred_element_type=F32,
            )
        term_s[:, p * 384 : (p + 1) * 384] = near
    groups = term_s.shape[0] // 128
    for i in range(groups):
        for j in range(4):
            to = pl.ds(pl.multiple_of((j * 8 + step * groups + i) * 16, 16), 16)
            at = 128 * i + 32 * (j ^ x)
            keep_ref[to] = term_s[pl.ds(pl.multiple_of(at + 16 * core, 16), 16)]
            send_ref[to] = term_s[pl.ds(pl.multiple_of(at + 16 * (1 - core), 16), 16)]


def weight_terms(place, near, far, grads):
    rows, width = near.shape
    columns = 192 * len(grads)
    tile = 256
    whole = pl.BlockSpec((rows, 384), lambda i: (0, 0))
    return pl.pallas_call(
        weight_kernel,
        grid=(width // tile,),
        in_specs=[pl.BlockSpec(memory_space=pltpu.SMEM)]
        + [pl.BlockSpec((rows, tile), lambda i: (0, i))] * 2
        + [whole] * len(grads),
        out_specs=[pl.BlockSpec((width // 2, columns), lambda i: (0, 0))] * 2,
        out_shape=[jax.ShapeDtypeStruct((width // 2, columns), F32)] * 2,
        scratch_shapes=[pltpu.VMEM((tile, columns), F32)],
        compiler_params=pltpu.CompilerParams(vmem_limit_bytes=32 * 2**20),
        cost_estimate=pl.CostEstimate(flops=1000, bytes_accessed=1000, transcendentals=0),
    )(place, near, far, *grads)


def pick(array, place, dim):
    first = lax.index_in_dim(array, 0, dim, keepdims=False)
    second = lax.index_in_dim(array, 1, dim, keepdims=False)
    return jnp.where(place == 0, first, second), jnp.where(place == 0, second, first)


def by_core(own, other, core):
    both = jnp.where(core == 0, jnp.stack([own, other], 2), jnp.stack([other, own], 2))
    return both.reshape(1024, own.shape[-1])


def ordered(own, other, place):
    return jnp.where(place == 0, jnp.concatenate([own, other], 0), jnp.concatenate([other, own], 0))


def on_device(tokens, qkv_weight, grad_attn, positions, slopes):
    z_hi, z_lo, y_hi = lax.axis_index("zh"), lax.axis_index("zl"), lax.axis_index("yh")
    x, core, head = lax.axis_index("x"), lax.axis_index("c"), lax.axis_index("h")
    rows = tokens.shape[0]
    third = rows // 3

    def local(array):
        first, second = array[:third], array[third : 2 * third]
        return jnp.where(head == 0, array, jnp.concatenate([second, first, array[2 * third :]], 0))

    with jax.named_scope("tokens"):
        got = [swap(lax.dynamic_slice_in_dim(tokens, head * third, third, 0), "zh"), swap(tokens[2 * third :], "zh")]

    with jax.named_scope("weights"):
        w = qkv_weight.reshape(16, 3, 2, 2, 128).transpose(2, 0, 3, 1, 4).reshape(2, 16, 768)
        mine = lax.dynamic_index_in_dim(w, z_hi, 0, keepdims=False)
        theirs = lax.dynamic_index_in_dim(w, 1 - z_hi, 0, keepdims=False)
        digits = jnp.stack([(positions >> shift) & 255 for shift in (16, 8, 0)]).astype(BF)
        other = lax.ppermute(jnp.concatenate([theirs, digits], 0), ("zh", "zl"), [(i, i ^ 2) for i in range(4)])
        pieces = [
            mine,
            lax.ppermute(mine, ("zh", "zl"), [(i, i ^ 1) for i in range(4)]),
            other[:16],
            lax.ppermute(theirs, ("zh", "zl"), [(i, i ^ 3) for i in range(4)]),
        ]
        digits = other[16:].astype(jnp.int32)
        far_positions = local((digits[0] << 16) + (digits[1] << 8) + digits[2])
        pos = jnp.concatenate([positions, far_positions], 0)
        logd = jnp.log((1 + jnp.abs(pos[:, None] - pos[None, :])).astype(F32))
        pieces = [jnp.where(z_lo == 0, pieces[i], pieces[i ^ 1]) for i in range(4)]
        pieces = [jnp.where(z_hi == 0, pieces[i], pieces[i ^ 2]) for i in range(4)]
        w, grad_attn = lax.optimization_barrier((jnp.stack(pieces)[:, None], grad_attn))
        other = swap(w, "yh")
        w = jnp.where(y_hi == 0, jnp.concatenate([w, other], 1), jnp.concatenate([other, w], 1)).reshape(8, 16, 768)
        w, logd = lax.optimization_barrier((w, logd))
        pieces = [w] + [lax.ppermute(w, "x", [(i, i ^ j) for i in range(4)]) for j in range(1, 4)]
        pieces[1], got[0] = lax.optimization_barrier((pieces[1], got[0]))
        relayed = swap(got[0], "h")
        pieces = [jnp.where((x & 1) == 0, pieces[i], pieces[i ^ 1]) for i in range(4)]
        pieces = [jnp.where((x & 2) == 0, pieces[i], pieces[i ^ 2]) for i in range(4)]
        w_core = jnp.stack(pieces, 1)
        w = by_core(w_core, swap(w_core, "c"), core)
        far_tokens = jnp.concatenate([got[0], relayed, got[1]], 0)

    with jax.named_scope("bias"):
        g_near = lax.dynamic_slice_in_dim(grad_attn, z_hi * 256, 256, 1)
        g_far = swap(local(lax.dynamic_slice_in_dim(grad_attn, (1 - z_hi) * 256, 256, 1)), "zh")
        slopes = lax.dynamic_slice_in_dim(slopes, z_hi * 4, 4, 0)

    with jax.named_scope("projection"):
        near = dot(tokens, w).astype(BF)
        far = dot(far_tokens, w).astype(BF)
    with jax.named_scope("attention"):
        near0, far0 = attention(head, slopes[:2], near, far, g_near, g_far, logd, 0, [rows])
        w_core, near = lax.optimization_barrier((w_core, near))
        w_other = swap(w_core, "zh")
        g_near, near0, w_other = lax.optimization_barrier((g_near, near0, w_other))
        near1, *far1 = attention(head, slopes[2:], near, far, g_near, g_far, logd, 1, [third, 2 * third])

    with jax.named_scope("d_tokens"):
        w_other = by_core(w_other, swap(w_other, "c"), core)
        back0 = swap(far0, "zh")
        back1 = [swap(part, "zh") for part in far1]
        base = dot(
            jnp.concatenate([near0, near1, back0], 1), jnp.concatenate([w, w_other[:, :384]], 1), ((1,), (1,))
        )
        mine = []
        for i in range(3):
            back = back1[0] if i == 0 else back1[1][(i - 1) * third : i * third]
            part = base[i * third : (i + 1) * third] + dot(back, w_other[:, 384:], ((1,), (1,)))
            mine.append(part.astype(BF))

    with jax.named_scope("d_weight"):
        far1 = jnp.concatenate(far1, 0)
        far1, back0, mine[0] = lax.optimization_barrier((far1, back0, mine[0]))
        keep, send = weight_terms(jnp.stack([core, x, head]), tokens, far_tokens, [near0, far0, near1, far1])
        other = swap(send, "c")
        theirs = [swap(mine[0], "h")]
        other, theirs[0] = lax.optimization_barrier((other, theirs[0]))
        term = (keep + other).reshape(4, 8, 16, 768)
        total = term[0]
        for j in range(1, 4):
            piece = lax.ppermute(term[j].astype(BF), "x", [(i, i ^ j) for i in range(4)])
            total = total + piece.astype(F32)
        total = total.reshape(2, 2, 2, 16, 768)
        theirs.append(swap(mine[1], "h"))
        total, theirs[1], mine[2] = lax.optimization_barrier((total, theirs[1], mine[2]))
        theirs.append(swap(mine[2], "h"))
        mine_w, their_w = pick(total, y_hi, 2)
        total = mine_w + swap(their_w.astype(BF), "yh").astype(F32)
        halves = []
        for a in range(2):
            part = total if a == 0 else total[::-1]
            part = jnp.where(z_hi == 0, part[0], part[1])
            mine_w, their_w = pick(part, z_lo, 0)
            if a:
                mine_w = lax.ppermute(mine_w, ("zh", "zl"), [(i, i ^ 2) for i in range(4)])
            halves.append(mine_w + lax.ppermute(their_w, ("zh", "zl"), [(i, i ^ (2 * a + 1)) for i in range(4)]))
        total = jnp.where(z_hi == 0, jnp.stack(halves), jnp.stack(halves[::-1]))
        d_weight = total.reshape(2, 16, 2, 3, 128).transpose(1, 3, 0, 2, 4).reshape(16, 3, 512)

    with jax.named_scope("d_tokens"):
        d_tokens = None
        for i in range(3):
            d_tokens = add_rows(d_tokens, mine[i], theirs[i], i, 3)
    return d_tokens, d_weight


def solution(mesh):
    mesh = jax.sharding.Mesh(mesh.devices.reshape(2, 2, 2, 4, 2, 2), ("zh", "zl", "yh", "x", "c", "h"))
    ctx = ("zh", "zl", "yh", "x", "c")
    return jax.shard_map(
        on_device,
        mesh=mesh,
        in_specs=(P(ctx, None), P(ctx, None, "h"), P(ctx, "h"), P(ctx), P("h")),
        out_specs=(P(ctx, None), P(ctx, None, "h")),
        check_vma=False,
    )
```

```python
import jax
import jax.numpy as jnp
from jax import lax
from jax.experimental import pallas as pl
from jax.experimental.pallas import tpu as pltpu
from jax.sharding import PartitionSpec as P

BF = jnp.bfloat16
F32 = jnp.float32
TILE = 512
CHUNK = 128


def swap(value, axis):
    return lax.ppermute(value, axis, [(0, 1), (1, 0)])


def dot(a, b, dims=((1,), (0,))):
    return lax.dot_general(a, b, (dims, ((), ())), preferred_element_type=F32)


def attention_kernel(
    place_ref, slopes_ref, qo, qf, ko, kf, vo, vf, go, gf, logd_ref, near_ref, *rest,
):
    *far_refs, q_s, k_s, v_s, g_s, kt_s, dq_s, dk_s, dv_s, s_s, dp_s = rest
    step = pl.program_id(0)
    rows = qo.shape[0]
    total = 2 * rows
    steps = total // TILE

    @pl.when(step == 0)
    def _():
        for scratch, near, far in ((q_s, qo, qf), (k_s, ko, kf), (v_s, vo, vf), (g_s, go, gf)):
            scratch[:rows] = near[...]
            scratch[rows:] = far[...]
        kt_s[...] = k_s[...].astype(F32).T.astype(BF)
        dk_s[...] = jnp.zeros_like(dk_s)
        dv_s[...] = jnp.zeros_like(dv_s)

    here = pl.ds(pl.multiple_of(step * TILE, TILE), TILE)
    q = q_s[here].astype(F32) * 0.125
    g = g_s[here].astype(F32)
    q_t, g_t = q.T, g.T
    upper = lax.broadcasted_iota(jnp.int32, (128, TILE), 0) < 64
    left = lax.broadcasted_iota(jnp.int32, (TILE, 128), 1) < 64
    zero = jnp.float32(0)
    qts = [jnp.where(upper, q_t, zero).astype(BF), jnp.where(upper, zero, q_t).astype(BF)]
    gts = [jnp.where(upper, g_t, zero).astype(BF), jnp.where(upper, zero, g_t).astype(BF)]
    qs = [jnp.where(left, q, zero).astype(BF), jnp.where(left, zero, q).astype(BF)]
    gs = [jnp.where(left, g, zero).astype(BF), jnp.where(left, zero, g).astype(BF)]
    top = [jnp.full((1, TILE), -jnp.inf, F32)] * 2
    norm = [jnp.zeros((1, TILE), F32)] * 2
    delta = [jnp.zeros((1, TILE), F32)] * 2
    inverse = [None] * 2
    dq_t = [jnp.zeros((64, TILE), F32)] * 2
    parts = [slice(c * CHUNK, (c + 1) * CHUNK) for c in range(total // CHUNK)]

    def scores(h, part):
        score = dot(k_s[part], qts[h]) - slopes_ref[h] * logd_ref[part]
        s_s[h, part] = score
        top[h] = jnp.maximum(top[h], jnp.max(score, axis=0, keepdims=True))

    def sums(h, part):
        e = jnp.exp(s_s[h, part] - top[h])
        s_s[h, part] = e
        dp = dot(v_s[part], gts[h])
        dp_s[h, part] = dp
        norm[h] += jnp.sum(e, axis=0, keepdims=True)
        delta[h] += jnp.sum(e * dp, axis=0, keepdims=True)

    def normalise(h):
        inverse[h] = 1.0 / norm[h]
        delta[h] = delta[h] * inverse[h]

    def products(h, part):
        p = s_s[h, part] * inverse[h]
        ds = (p * (dp_s[h, part] - delta[h])).astype(BF)
        dv_s[part] += dot(p.astype(BF), gs[h])
        dk_s[part] += dot(ds, qs[h])
        dq_t[h] += dot(kt_s[h * 64 : (h + 1) * 64, part], ds)

    for part in parts:
        scores(0, part)
    for part in parts:
        sums(0, part)
        scores(1, part)
    normalise(0)
    for part in parts:
        products(0, part)
        sums(1, part)
    normalise(1)
    for part in parts:
        products(1, part)
    dq = jnp.concatenate(dq_t, 0).T * 0.125
    dq_s[here] = dq.astype(BF)

    @pl.when(step == steps - 1)
    def _():
        near_ref[:, :128] = dq_s[:rows]
        near_ref[:, 128:256] = dk_s[:rows].astype(BF)
        near_ref[:, 256:384] = dv_s[:rows].astype(BF)
        third = rows // 3
        first = 0
        for far_ref in far_refs:
            for k in range(far_ref.shape[0] // third):
                at = (first + k) ^ place_ref[0] if first + k < 2 else first + k
                part = pl.ds(pl.multiple_of(rows + at * third, 64), third)
                mine = slice(k * third, (k + 1) * third)
                far_ref[mine, :128] = dq_s[part]
                far_ref[mine, 128:256] = dk_s[part].astype(BF)
                far_ref[mine, 256:384] = dv_s[part].astype(BF)
            first += far_ref.shape[0] // third


def attention(place, slopes, near, far, g_near, g_far, logd, pair, pieces):
    rows = near.shape[0]
    total = 2 * rows
    sizes = [rows] + pieces

    def column(block):
        return pl.BlockSpec((rows, 128), lambda t: (0, block))

    specs = []
    for c in range(3):
        specs += [column(3 * pair + c)] * 2
    return pl.pallas_call(
        attention_kernel,
        grid=(total // TILE,),
        in_specs=[pl.BlockSpec(memory_space=pltpu.SMEM)] * 2
        + specs
        + [column(pair)] * 2
        + [pl.BlockSpec((total, TILE), lambda t: (0, t))],
        out_specs=[pl.BlockSpec((n, 384), lambda t: (0, 0)) for n in sizes],
        out_shape=[jax.ShapeDtypeStruct((n, 384), BF) for n in sizes],
        scratch_shapes=[pltpu.VMEM((total, 128), BF)] * 4
        + [pltpu.VMEM((128, total), BF), pltpu.VMEM((total, 128), BF)]
        + [pltpu.VMEM((total, 128), F32)] * 2
        + [pltpu.VMEM((2, total, TILE), F32)] * 2,
        compiler_params=pltpu.CompilerParams(vmem_limit_bytes=44 * 2**20),
        cost_estimate=pl.CostEstimate(
            flops=2 * 5 * 2 * total * total * 256, bytes_accessed=4 * total * total, transcendentals=2 * total * total
        ),
    )(place[None], slopes, near, far, near, far, near, far, g_near, g_far, logd)


def add_kernel(mine_ref, theirs_ref, *refs):
    refs[-1][...] = (mine_ref[...].astype(F32) + theirs_ref[...].astype(F32)).astype(BF)


def add_rows(out, mine, theirs, index, count):
    rows, width = mine.shape
    return pl.pallas_call(
        add_kernel,
        grid=(1,),
        in_specs=[pl.BlockSpec((rows, width), lambda i: (0, 0))] * 2
        + ([] if out is None else [pl.BlockSpec(memory_space=pl.ANY)]),
        out_specs=pl.BlockSpec((rows, width), lambda i: (index, 0)),
        out_shape=jax.ShapeDtypeStruct((rows * count, width), BF),
        input_output_aliases={} if out is None else {2: 0},
        cost_estimate=pl.CostEstimate(flops=1000, bytes_accessed=1000, transcendentals=0),
    )(mine, theirs, *([] if out is None else [out]))


def weight_kernel(place_ref, near_ref, far_ref, *refs):
    *grads, keep_ref, send_ref, term_s = refs
    core, x, head = place_ref[0], place_ref[1], place_ref[2]
    step = pl.program_id(0)
    third = far_ref.shape[0] // 3
    for p in range(len(grads) // 2):
        near = lax.dot_general(near_ref[...], grads[2 * p][...], (((0,), (0,)), ((), ())), preferred_element_type=F32)
        for k in range(3):
            at = k ^ head if k < 2 else k
            part = pl.ds(pl.multiple_of(at * third, 64), third)
            near += lax.dot_general(
                far_ref[k * third : (k + 1) * third],
                grads[2 * p + 1][part],
                (((0,), (0,)), ((), ())),
                preferred_element_type=F32,
            )
        term_s[:, p * 384 : (p + 1) * 384] = near
    groups = term_s.shape[0] // 128
    for i in range(groups):
        for j in range(4):
            to = pl.ds(pl.multiple_of((j * 8 + step * groups + i) * 16, 16), 16)
            at = 128 * i + 32 * (j ^ x)
            keep_ref[to] = term_s[pl.ds(pl.multiple_of(at + 16 * core, 16), 16)]
            send_ref[to] = term_s[pl.ds(pl.multiple_of(at + 16 * (1 - core), 16), 16)]


def weight_terms(place, near, far, grads):
    rows, width = near.shape
    columns = 192 * len(grads)
    tile = 256
    whole = pl.BlockSpec((rows, 384), lambda i: (0, 0))
    return pl.pallas_call(
        weight_kernel,
        grid=(width // tile,),
        in_specs=[pl.BlockSpec(memory_space=pltpu.SMEM)]
        + [pl.BlockSpec((rows, tile), lambda i: (0, i))] * 2
        + [whole] * len(grads),
        out_specs=[pl.BlockSpec((width // 2, columns), lambda i: (0, 0))] * 2,
        out_shape=[jax.ShapeDtypeStruct((width // 2, columns), F32)] * 2,
        scratch_shapes=[pltpu.VMEM((tile, columns), F32)],
        compiler_params=pltpu.CompilerParams(vmem_limit_bytes=32 * 2**20),
        cost_estimate=pl.CostEstimate(flops=1000, bytes_accessed=1000, transcendentals=0),
    )(place, near, far, *grads)


def pick(array, place, dim):
    first = lax.index_in_dim(array, 0, dim, keepdims=False)
    second = lax.index_in_dim(array, 1, dim, keepdims=False)
    return jnp.where(place == 0, first, second), jnp.where(place == 0, second, first)


def by_core(own, other, core):
    both = jnp.where(core == 0, jnp.stack([own, other], 2), jnp.stack([other, own], 2))
    return both.reshape(1024, own.shape[-1])


def ordered(own, other, place):
    return jnp.where(place == 0, jnp.concatenate([own, other], 0), jnp.concatenate([other, own], 0))


def on_device(tokens, qkv_weight, grad_attn, positions, slopes):
    z_hi, z_lo, y_hi = lax.axis_index("zh"), lax.axis_index("zl"), lax.axis_index("yh")
    x, core, head = lax.axis_index("x"), lax.axis_index("c"), lax.axis_index("h")
    rows = tokens.shape[0]
    third = rows // 3

    def local(array):
        first, second = array[:third], array[third : 2 * third]
        return jnp.where(head == 0, array, jnp.concatenate([second, first, array[2 * third :]], 0))

    with jax.named_scope("tokens"):
        got = [swap(lax.dynamic_slice_in_dim(tokens, head * third, third, 0), "zh"), swap(tokens[2 * third :], "zh")]

    with jax.named_scope("weights"):
        w = qkv_weight.reshape(16, 3, 2, 2, 128).transpose(2, 0, 3, 1, 4).reshape(2, 16, 768)
        mine = lax.dynamic_index_in_dim(w, z_hi, 0, keepdims=False)
        theirs = lax.dynamic_index_in_dim(w, 1 - z_hi, 0, keepdims=False)
        digits = jnp.stack([(positions >> shift) & 255 for shift in (16, 8, 0)]).astype(BF)
        other = lax.ppermute(jnp.concatenate([theirs, digits], 0), ("zh", "zl"), [(i, i ^ 2) for i in range(4)])
        pieces = [
            mine,
            lax.ppermute(mine, ("zh", "zl"), [(i, i ^ 1) for i in range(4)]),
            other[:16],
            lax.ppermute(theirs, ("zh", "zl"), [(i, i ^ 3) for i in range(4)]),
        ]
        digits = other[16:].astype(jnp.int32)
        far_positions = local((digits[0] << 16) + (digits[1] << 8) + digits[2])
        pos = jnp.concatenate([positions, far_positions], 0)
        logd = jnp.log((1 + jnp.abs(pos[:, None] - pos[None, :])).astype(F32))
        pieces = [jnp.where(z_lo == 0, pieces[i], pieces[i ^ 1]) for i in range(4)]
        pieces = [jnp.where(z_hi == 0, pieces[i], pieces[i ^ 2]) for i in range(4)]
        w, grad_attn = lax.optimization_barrier((jnp.stack(pieces)[:, None], grad_attn))
        other = swap(w, "yh")
        w = jnp.where(y_hi == 0, jnp.concatenate([w, other], 1), jnp.concatenate([other, w], 1)).reshape(8, 16, 768)
        w, logd = lax.optimization_barrier((w, logd))
        pieces = [w] + [lax.ppermute(w, "x", [(i, i ^ j) for i in range(4)]) for j in range(1, 4)]
        pieces[1], got[0] = lax.optimization_barrier((pieces[1], got[0]))
        relayed = swap(got[0], "h")
        pieces = [jnp.where((x & 1) == 0, pieces[i], pieces[i ^ 1]) for i in range(4)]
        pieces = [jnp.where((x & 2) == 0, pieces[i], pieces[i ^ 2]) for i in range(4)]
        w_core = jnp.stack(pieces, 1)
        w = by_core(w_core, swap(w_core, "c"), core)
        far_tokens = jnp.concatenate([got[0], relayed, got[1]], 0)

    with jax.named_scope("bias"):
        g_near = lax.dynamic_slice_in_dim(grad_attn, z_hi * 256, 256, 1)
        g_far = swap(local(lax.dynamic_slice_in_dim(grad_attn, (1 - z_hi) * 256, 256, 1)), "zh")
        slopes = lax.dynamic_slice_in_dim(slopes, z_hi * 4, 4, 0)

    with jax.named_scope("projection"):
        near = dot(tokens, w).astype(BF)
        far = dot(far_tokens, w).astype(BF)
    with jax.named_scope("attention"):
        near0, far0 = attention(head, slopes[:2], near, far, g_near, g_far, logd, 0, [rows])
        w_core, near = lax.optimization_barrier((w_core, near))
        w_other = swap(w_core, "zh")
        g_near, near0, w_other = lax.optimization_barrier((g_near, near0, w_other))
        near1, *far1 = attention(head, slopes[2:], near, far, g_near, g_far, logd, 1, [third, 2 * third])

    with jax.named_scope("d_tokens"):
        w_other = by_core(w_other, swap(w_other, "c"), core)
        back0 = swap(far0, "zh")
        back1 = [swap(part, "zh") for part in far1]
        base = dot(
            jnp.concatenate([near0, near1, back0], 1), jnp.concatenate([w, w_other[:, :384]], 1), ((1,), (1,))
        )
        mine = []
        for i in range(3):
            back = back1[0] if i == 0 else back1[1][(i - 1) * third : i * third]
            part = base[i * third : (i + 1) * third] + dot(back, w_other[:, 384:], ((1,), (1,)))
            mine.append(part.astype(BF))

    with jax.named_scope("d_weight"):
        far1 = jnp.concatenate(far1, 0)
        far1, back0 = lax.optimization_barrier((far1, back0))
        keep, send = weight_terms(jnp.stack([core, x, head]), tokens, far_tokens, [near0, far0, near1, far1])
        other = swap(send, "c")
        theirs = [swap(mine[0], "h")]
        term = (keep + other).reshape(4, 8, 16, 768)
        total = term[0]
        for j in range(1, 4):
            piece = lax.ppermute(term[j].astype(BF), "x", [(i, i ^ j) for i in range(4)])
            total = total + piece.astype(F32)
        total = total.reshape(2, 2, 2, 16, 768)
        theirs.append(swap(mine[1], "h"))
        total, theirs[0] = lax.optimization_barrier((total, theirs[0]))
        theirs.append(swap(mine[2], "h"))
        mine_w, their_w = pick(total, y_hi, 2)
        total = mine_w + swap(their_w.astype(BF), "yh").astype(F32)
        total, theirs[1] = lax.optimization_barrier((total, theirs[1]))
        halves = []
        for a in range(2):
            part = total if a == 0 else total[::-1]
            part = jnp.where(z_hi == 0, part[0], part[1])
            mine_w, their_w = pick(part, z_lo, 0)
            if a:
                mine_w = lax.ppermute(mine_w, ("zh", "zl"), [(i, i ^ 2) for i in range(4)])
            halves.append(mine_w + lax.ppermute(their_w, ("zh", "zl"), [(i, i ^ (2 * a + 1)) for i in range(4)]))
        total = jnp.where(z_hi == 0, jnp.stack(halves), jnp.stack(halves[::-1]))
        d_weight = total.reshape(2, 16, 2, 3, 128).transpose(1, 3, 0, 2, 4).reshape(16, 3, 512)

    with jax.named_scope("d_tokens"):
        d_tokens = None
        for i in range(3):
            d_tokens = add_rows(d_tokens, mine[i], theirs[i], i, 3)
    return d_tokens, d_weight


def solution(mesh):
    mesh = jax.sharding.Mesh(mesh.devices.reshape(2, 2, 2, 4, 2, 2), ("zh", "zl", "yh", "x", "c", "h"))
    ctx = ("zh", "zl", "yh", "x", "c")
    return jax.shard_map(
        on_device,
        mesh=mesh,
        in_specs=(P(ctx, None), P(ctx, None, "h"), P(ctx, "h"), P(ctx), P("h")),
        out_specs=(P(ctx, None), P(ctx, None, "h")),
        check_vma=False,
    )
```
